32 devices in a mesh: groups: 2 (over y), blk: 4 (over z), sub: 4 (over x, core).
Axes of the slice: x: 2, y: 2, z: 4, core: 2. Of those that a mesh axis runs over, the one named last changes fastest.
Arguments:
- user_factors: float32 [256, 8192], P('sub', ('groups', 'blk')), parts along dimension 1, may hold values from -1.5 to 1.5
- item_factors: float32 [256, 8192], P('sub', ('groups', 'blk')), parts along dimension 1, may hold values from -1.5 to 1.5
- ratings: bfloat16 [4, 8192, 1024], P(None, ('groups', 'blk')), parts along dimension 1, may hold values from -6 to 6
- counts: int32 [4, 8192, 8], P(None, ('groups', 'blk')), parts along dimension 1, may hold values from 0 to 128
- occupancy: int32 [4, 64, 8], P(None, ('groups', 'blk')), parts along dimension 1, may hold values from 0 to 1
Outputs:
- users_after: float32 [256, 8192], P('sub', ('groups', 'blk')), parts along dimension 1
- items_after: float32 [256, 8192], P('sub', ('groups', 'blk')), parts along dimension 1
The draws below stay inside these ranges and needn't reach their ends.
There are 2 independent parts, one for each index of `groups`. The reference program is written for one: setup_inputs(seed, part) draws one part's arguments, and reference() takes and returns one part's arrays. A program takes and returns all parts, laid end to end along the dimension named above; each array names one. Nothing has to cross between parts.
All inputs are finite; a program needn't handle non-finite values.
Results may differ from the reference program's by a relative error of at most 0.0025.
Values may be sent and summed in bfloat16 or wider, within the bound.
A program may use at most 64 MiB of HBM per device.

```python
import jax
import jax.numpy as jnp
from jax import lax

R = 256
USERS_DEV = 1024
ITEM_BLOCK = 1024
STRATA = 4
USERS = 4096
ITEMS = 4096
N_BLK = 4


def draw_occupancy(key, part):
    key = jax.random.fold_in(key, 11)
    first_key, second_key = jax.random.split(key)
    level = jax.random.randint(first_key, (STRATA, USERS // 128, 1), 1, 9)
    coins = jax.random.randint(second_key, (STRATA, USERS // 128, ITEM_BLOCK // 128), 0, 8)
    return (coins < level).astype(jnp.int32)


def plant(values, rng, least, largest):
    index_at = [jax.random.randint(jax.random.fold_in(rng, axis), (), 0, length) for axis, length in enumerate(values.shape)]
    widest = values.shape.index(max(values.shape))
    next_to = index_at[:widest] + [(index_at[widest] + 1) % values.shape[widest]] + index_at[widest + 1:]
    return values.at[tuple(index_at)].set(least).at[tuple(next_to)].set(largest)


def block_scale(own_key, dims, shards, smallest, top_value):
    factor_of, own = 1.0, jax.random.fold_in(own_key, 6)
    for axis_at, shards_of in shards:
        heights = jnp.exp(jax.random.uniform(jax.random.fold_in(own, axis_at), (shards_of,), jnp.float32, smallest / len(shards), top_value / len(shards)))
        factor_of = factor_of * jnp.repeat(heights, dims[axis_at] // shards_of).reshape([-1 if axis == axis_at else 1 for axis in range(len(dims))])
    return factor_of


def noise(key, dims, deviation, most, cuts=(), kind=jnp.bfloat16):
    entries = deviation * jax.random.normal(key, dims, jnp.float32)
    if cuts:
        entries = entries * block_scale(key, dims, cuts, -0.22, 0.18)
    return jnp.clip(entries, -most, most).astype(kind)


def setup_inputs(seed: int = 0, part: int = 0) -> dict:
    key_list = jax.random.split(jax.random.key(seed), 6)
    own_keys = jax.random.split(jax.random.fold_in(key_list[5], part), 6)
    return {
        "user_factors": noise(own_keys[0], (R, USERS), 0.25, 1.5, ((0, 4), (1, 4)), jnp.float32),
        "item_factors": noise(own_keys[1], (R, ITEMS), 0.25, 1.5, ((0, 4), (1, 4)), jnp.float32),
        "ratings": noise(own_keys[2], (STRATA, USERS, ITEM_BLOCK), 1.0, 6.0, ((1, 4),)),
        "counts": plant(jax.random.randint(own_keys[3], (STRATA, USERS, ITEM_BLOCK // 128), 0, 129), jax.random.fold_in(own_keys[3], 1), 0, 128).astype(jnp.int32),
        "occupancy": draw_occupancy(jax.random.fold_in(jax.random.fold_in(key_list[5], part), 71), part),
    }


step_rate = 0.02


def weights_of(counts, occupied):
    row_count, tile_count = counts.shape
    lane_index = jnp.arange(128, dtype=jnp.int32)
    inside = (lane_index[None, None, :] < counts[:, :, None]).astype(jnp.float32)
    spread = jnp.broadcast_to(occupied[:, None, :, None].astype(jnp.float32), (row_count // 128, 128, tile_count, 128))
    return inside.reshape(row_count, tile_count * 128) * spread.reshape(row_count, tile_count * 128)


def rounded(value):
    return lax.optimization_barrier(value.astype(jnp.bfloat16)).astype(jnp.float32)


def reference(user_factors, item_factors, ratings, counts, occupancy):
    user_state = user_factors.reshape(R, N_BLK, USERS_DEV)
    item_state = item_factors.reshape(R, N_BLK, ITEM_BLOCK)
    exact = lax.Precision.HIGHEST
    for stratum in range(STRATA):
        weight = weights_of(counts[stratum], occupancy[stratum]).reshape(N_BLK, USERS_DEV, ITEM_BLOCK)
        low_users = rounded(user_state)
        low_items = rounded(item_state)
        scores = jnp.einsum("rbu,rbi->bui", low_users, low_items, precision=exact)
        target = ratings[stratum].astype(jnp.float32).reshape(N_BLK, USERS_DEV, ITEM_BLOCK)
        errors = rounded(weight * (scores - target))
        new_users = user_state - step_rate * jnp.einsum("rbi,bui->rbu", low_items, errors, precision=exact)
        item_state = item_state - step_rate * jnp.einsum("rbu,bui->rbi", low_users, errors, precision=exact)
        user_state = new_users
        item_state = jnp.roll(item_state, 1, axis=1)
    return user_state.reshape(R, USERS), item_state.reshape(R, ITEMS)
```

```python
import functools

import jax
import jax.numpy as jnp
from jax import lax
from jax.experimental import pallas as pl
from jax.experimental.pallas import tpu as pltpu
from jax.sharding import PartitionSpec as P

step_rate = 0.02
LO = 2
CHUNKS = 2
PARTS = 2
F32, BF16 = jnp.float32, jnp.bfloat16


def dot_nn(a, b):
    return lax.dot_general(a, b, (((1,), (0,)), ((), ())), preferred_element_type=F32)


def dot_nt(a, b):
    return lax.dot_general(a, b, (((1,), (1,)), ((), ())), preferred_element_type=F32)


def kernel(
    n_blk, n_sub, strata,
    users_ref, items_ref, counts_ref, occ_ref, ratings_ref,
    users_out, items_out,
    low_u, rest_u, low_ut, state_u, part_s, part_r, last_s, last_r,
    own_i, own_rest, slots, rests, hop_s, hop_rest, final_s, final_r, errors, rat, weight,
    rat_sem, u_s, u_r, v_s, v_r, i_s, i_r, j_s, j_r, z_s, z_r, y_s, y_r, f_s, f_r, g_s, g_r, p_s, p_r,
):
    n_hi = n_sub // LO
    rows, users = users_ref.shape
    ranks = rows * n_sub
    items = items_ref.shape[1]
    half = items // LO
    width = half // CHUNKS
    pair = LO * rows
    part = users // PARTS
    blk = lax.axis_index("blk")
    me = lax.axis_index("sub")
    hi, lo = me // LO, me % LO

    def at_blk(steps):
        return lax.rem(blk + steps % n_blk, n_blk)

    def at_hi(steps):
        return lax.rem(hi + steps, n_hi)

    def at_lo(steps):
        return lax.rem(lo + steps, LO)

    def sub_of(hi_at, lo_at):
        return hi_at * LO + lo_at

    def rows_of(sub_at):
        return pl.ds(pl.multiple_of(sub_at * rows, rows), rows)

    def pair_of(hi_at):
        return pl.ds(pl.multiple_of(hi_at * pair, pair), pair)

    def send(src, dst, send_sem, recv_sem, blk_at, sub_at):
        copy = pltpu.make_async_remote_copy(
            src_ref=src, dst_ref=dst, send_sem=send_sem, recv_sem=recv_sem,
            device_id={"blk": blk_at, "sub": sub_at}, device_id_type=pl.DeviceIdType.MESH,
        )
        copy.start()
        return copy

    def arrived(dst, recv_sem):
        pltpu.make_async_remote_copy(
            src_ref=dst, dst_ref=dst, send_sem=recv_sem, recv_sem=recv_sem,
            device_id={"blk": blk, "sub": me}, device_id_type=pl.DeviceIdType.MESH,
        ).wait_recv()

    sent = []
    loads = []
    for s in range(strata):
        load = pltpu.make_async_copy(
            ratings_ref.at[s, :, pl.ds(pl.multiple_of(lo * half, half), half)],
            rat.at[s], rat_sem.at[s],
        )
        load.start()
        loads.append(load)

    barrier = pltpu.get_barrier_semaphore()
    greeted = [(0, dh, dl) for dh in range(n_hi) for dl in range(LO) if (dh, dl) != (0, 0)]
    for d in sorted({sign * k % n_blk for k in (1,) for sign in (1, -1)} - {0}):
        greeted += [(d, 0, dl) for dl in range(LO)]
    for d, dh, dl in greeted:
        pl.semaphore_signal(
            barrier, inc=1,
            device_id={"blk": at_blk(d), "sub": sub_of(at_hi(dh), at_lo(dl))},
            device_id_type=pl.DeviceIdType.MESH,
        )

    def split(value):
        high = value.astype(BF16)
        return high, (value - high.astype(F32)).astype(BF16)

    low_u[rows_of(me), :], rest_u[rows_of(me), :] = split(users_ref[...])
    for h in range(LO):
        for k in range(CHUNKS):
            cols = slice((h * CHUNKS + k) * width, (h * CHUNKS + k + 1) * width)
            own_i[h, k], own_rest[h, k] = split(items_ref[:, cols])
    for k in range(CHUNKS):
        slots[0, k, rows_of(me), :] = own_i[lo, k]
        rests[0, k, rows_of(me), :] = own_rest[lo, k]
    pl.semaphore_wait(barrier, len(greeted))

    mine = low_u.at[rows_of(me), :]
    for dh in range(1, n_hi):
        sent.append(send(mine, mine, u_s.at[dh], u_r.at[me], blk, sub_of(at_hi(dh), lo)))
    sent.append(send(mine, mine, u_s.at[0], u_r.at[me], blk, sub_of(hi, at_lo(1))))
    user_sent = list(sent)
    sent.clear()
    for k in range(CHUNKS):
        at = 0
        for dl in range(LO):
            for dh in range(n_hi):
                if (dh, dl) == (0, 0):
                    continue
                sent.append(send(
                    own_i.at[at_lo(dl), k], slots.at[0, k, rows_of(me), :],
                    i_s.at[k, at], i_r.at[k, me], blk, sub_of(at_hi(dh), at_lo(dl)),
                ))
                at += 1
    mine = rest_u.at[rows_of(me), :]
    for dh in range(1, n_hi):
        sent.append(send(mine, mine, v_s.at[dh], v_r.at[me], blk, sub_of(at_hi(dh), lo)))
    sent.append(send(mine, mine, v_s.at[0], v_r.at[me], blk, sub_of(hi, at_lo(1))))
    for k in range(CHUNKS):
        sent.append(send(
            own_rest.at[at_lo(1), k], rests.at[0, k, rows_of(me), :],
            j_s.at[k], j_r.at[k], blk, sub_of(hi, at_lo(1)),
        ))

    tiles = counts_ref.shape[2]
    group = users // occ_ref.shape[1]
    tile_width = items // tiles
    tile_at = lax.broadcasted_iota(jnp.int32, (tiles, half), 0)
    lane_at = lax.broadcasted_iota(jnp.int32, (tiles, half), 1)
    spread = jnp.where((lane_at + lo * half) // tile_width == tile_at, 1.0, 0.0).astype(BF16)
    position = (lax.broadcasted_iota(jnp.int32, (group, half), 1) % tile_width).astype(F32)

    def make_weight(s):
        for b in range(users // group):
            seen = counts_ref[s, b * group:(b + 1) * group, :] * occ_ref[s, b:b + 1, :]
            seen = dot_nn(seen.astype(F32).astype(BF16), spread)
            weight[s, b * group:(b + 1) * group, :] = jnp.where(position < seen, 1.0, 0.0).astype(BF16)

    make_weight(0)
    for dh in range(1, n_hi):
        other = sub_of(at_hi(dh), lo)
        piece = low_u.at[rows_of(other), :]
        arrived(piece, u_r.at[other])
        user_sent.append(send(piece, piece, u_s.at[n_hi - 1 + dh], u_r.at[other], blk, sub_of(hi, at_lo(1))))
    for s in range(1, strata):
        make_weight(s)
    for dh in range(n_hi):
        other = sub_of(at_hi(dh), at_lo(1))
        arrived(low_u.at[rows_of(other), :], u_r.at[other])
    low_ut[...] = low_u[...].T

    def pass_on(s, k):
        arrived(slots.at[s, k, pair_of(hi), :], z_r.at[s, k])
        piece = slots.at[s, k, pair_of(hi), :]
        for dh in range(1, n_hi):
            sent.append(send(piece, piece, f_s.at[s, k, dh], f_r.at[s, k, hi], blk, sub_of(at_hi(dh), lo)))

    for s in range(strata):
        last = s == strata - 1
        loads[s].wait()
        for k in range(CHUNKS):
            if s == 0:
                for dh in range(n_hi):
                    for dl in range(LO):
                        if (dh, dl) != (0, 0):
                            other = sub_of(at_hi(dh), at_lo(dl))
                            arrived(slots.at[0, k, rows_of(other), :], i_r.at[k, other])
            else:
                if k > 0:
                    pass_on(s, k)
                for dh in range(1, n_hi):
                    other = at_hi(dh)
                    arrived(slots.at[s, k, pair_of(other), :], f_r.at[s, k, other])
            cols = slice(k * width, (k + 1) * width)
            scores = dot_nn(low_ut[...], slots[s, k])
            error = (scores - rat[s, :, cols].astype(F32)).astype(BF16) * weight[s, :, cols]
            errors[:, cols] = error
            step = step_rate * dot_nn(low_u[pair_of(hi), :], error)
            if s == 0:
                arrived(rests.at[0, k, rows_of(sub_of(hi, at_lo(1))), :], j_r.at[k])
            else:
                arrived(rests.at[s, k, pair_of(hi), :], y_r.at[s, k])
            after = slots[s, k, pair_of(hi), :].astype(F32) + rests[s, k, pair_of(hi), :].astype(F32) - step
            if not last:
                hop_s[s, k], hop_rest[s, k] = split(after)
                sent.append(send(
                    hop_s.at[s, k], slots.at[s + 1, k, pair_of(hi), :],
                    z_s.at[s, k], z_r.at[s + 1, k], at_blk(1), me,
                ))
            else:
                for h in range(LO):
                    final_s[k, h] = after[h * rows:(h + 1) * rows, :]
                for dl in range(LO):
                    sent.append(send(
                        final_s.at[k, at_lo(dl)], final_r.at[lo, k],
                        g_s.at[k, dl], g_r.at[lo, k], at_blk(1), sub_of(hi, at_lo(dl)),
                    ))
        if not last:
            for k in range(CHUNKS):
                sent.append(send(
                    hop_rest.at[s, k], rests.at[s + 1, k, pair_of(hi), :],
                    y_s.at[s, k], y_r.at[s + 1, k], at_blk(1), me,
                ))
        for p in range(PARTS):
            of_part = slice(p * part, (p + 1) * part)
            total = None
            for k in range(CHUNKS):
                held = slots[s, k] if not last else slots[s, k, pair_of(hi), :]
                grad = dot_nt(held, errors[of_part, k * width:(k + 1) * width])
                total = grad if total is None else total + grad
            if not last:
                part_s[s, p] = total
                sent.append(send(
                    part_s.at[s, p], part_r.at[s, p], p_s.at[s, p], p_r.at[s, p],
                    blk, sub_of(hi, at_lo(1)),
                ))
            else:
                for h in range(LO):
                    last_s[p, h] = total[h * rows:(h + 1) * rows, :]
                sent.append(send(
                    last_s.at[p, at_lo(1)], last_r.at[p], p_s.at[s, p], p_r.at[s, p],
                    blk, sub_of(hi, at_lo(1)),
                ))
        if s == 0:
            for dh in range(1, n_hi):
                other = sub_of(at_hi(dh), lo)
                piece = rest_u.at[rows_of(other), :]
                arrived(piece, v_r.at[other])
                sent.append(send(
                    piece, piece, v_s.at[n_hi - 1 + dh], v_r.at[other], blk, sub_of(hi, at_lo(1)),
                ))
            for dh in range(n_hi):
                other = sub_of(at_hi(dh), at_lo(1))
                arrived(rest_u.at[rows_of(other), :], v_r.at[other])
            for copy in user_sent:
                copy.wait_send()
        if not last:
            pass_on(s + 1, 0)
        for p in range(PARTS):
            of_part = slice(p * part, (p + 1) * part)
            if not last:
                arrived(part_r.at[s, p], p_r.at[s, p])
                before = state_u[:, of_part]
                if s == 0:
                    before = low_u[:, of_part].astype(F32) + rest_u[:, of_part].astype(F32)
                after = before - step_rate * (part_s[s, p] + part_r[s, p])
                state_u[:, of_part] = after
                after = after.astype(BF16)
                low_u[:, of_part] = after
                low_ut[of_part, :] = after.T
            else:
                arrived(last_r.at[p], p_r.at[s, p])
                users_out[:, of_part] = state_u[rows_of(me), of_part] - step_rate * (last_s[p, lo] + last_r[p])

    for dl in range(LO):
        for k in range(CHUNKS):
            arrived(final_r.at[at_lo(dl), k], g_r.at[at_lo(dl), k])
    for h in range(LO):
        for k in range(CHUNKS):
            items_out[:, (h * CHUNKS + k) * width:(h * CHUNKS + k + 1) * width] = final_r[h, k]
    for copy in sent:
        copy.wait_send()


def per_device(n_blk, n_sub, user_factors, item_factors, ratings, counts, occupancy):
    strata, users, items = ratings.shape
    rows = user_factors.shape[0]
    ranks = rows * n_sub
    half = items // LO
    width = half // CHUNKS
    pair = LO * rows
    n_hi = n_sub // LO
    part = users // PARTS
    vmem = pl.BlockSpec(memory_space=pltpu.VMEM)
    dma = pltpu.SemaphoreType.DMA
    return pl.pallas_call(
        functools.partial(kernel, n_blk, n_sub, strata),
        out_shape=(
            jax.ShapeDtypeStruct((rows, users), F32),
            jax.ShapeDtypeStruct((rows, items), F32),
        ),
        in_specs=[vmem] * 4 + [pl.BlockSpec(memory_space=pl.ANY)],
        out_specs=(vmem, vmem),
        scratch_shapes=[
            pltpu.VMEM((ranks, users), BF16),
            pltpu.VMEM((ranks, users), BF16),
            pltpu.VMEM((users, ranks), BF16),
            pltpu.VMEM((ranks, users), F32),
            pltpu.VMEM((strata - 1, PARTS, ranks, part), F32),
            pltpu.VMEM((strata - 1, PARTS, ranks, part), F32),
            pltpu.VMEM((PARTS, LO, rows, part), F32),
            pltpu.VMEM((PARTS, rows, part), F32),
            pltpu.VMEM((LO, CHUNKS, rows, width), BF16),
            pltpu.VMEM((LO, CHUNKS, rows, width), BF16),
            pltpu.VMEM((strata, CHUNKS, ranks, width), BF16),
            pltpu.VMEM((strata, CHUNKS, ranks, width), BF16),
            pltpu.VMEM((strata - 1, CHUNKS, pair, width), BF16),
            pltpu.VMEM((strata - 1, CHUNKS, pair, width), BF16),
            pltpu.VMEM((CHUNKS, LO, rows, width), F32),
            pltpu.VMEM((LO, CHUNKS, rows, width), F32),
            pltpu.VMEM((users, half), BF16),
            pltpu.VMEM((strata, users, half), BF16),
            pltpu.VMEM((strata, users, half), BF16),
            dma((strata,)),
            dma((2 * n_hi,)),
            dma((n_sub,)),
            dma((2 * n_hi,)),
            dma((n_sub,)),
            dma((CHUNKS, n_sub)),
            dma((CHUNKS, n_sub)),
            dma((CHUNKS,)),
            dma((CHUNKS,)),
            dma((strata, CHUNKS)),
            dma((strata, CHUNKS)),
            dma((strata, CHUNKS)),
            dma((strata, CHUNKS)),
            dma((strata, CHUNKS, n_hi)),
            dma((strata, CHUNKS, n_hi)),
            dma((CHUNKS, LO)),
            dma((LO, CHUNKS)),
            dma((strata, PARTS)),
            dma((strata, PARTS)),
        ],
        compiler_params=pltpu.CompilerParams(
            collective_id=0, has_side_effects=True, vmem_limit_bytes=52 * 2**20
        ),
        cost_estimate=pl.CostEstimate(
            flops=6 * strata * ranks * users * half, transcendentals=0,
            bytes_accessed=strata * users * items * 2,
        ),
    )(user_factors, item_factors, counts, occupancy, ratings)


def solution(mesh):
    return jax.shard_map(
        functools.partial(per_device, mesh.shape["blk"], mesh.shape["sub"]),
        mesh=mesh,
        in_specs=(
            P("sub", ("groups", "blk")),
            P("sub", ("groups", "blk")),
            P(None, ("groups", "blk"), None),
            P(None, ("groups", "blk"), None),
            P(None, ("groups", "blk"), None),
        ),
        out_specs=(P("sub", ("groups", "blk")), P("sub", ("groups", "blk"))),
        check_vma=False,
    )
```

```python
import functools

import jax
import jax.numpy as jnp
from jax import lax
from jax.experimental import pallas as pl
from jax.experimental.pallas import tpu as pltpu
from jax.sharding import PartitionSpec as P

step_rate = 0.02
LO = 2
CHUNKS = 2
PIECES = 1
PARTS = 2
F32, BF16 = jnp.float32, jnp.bfloat16


def dot_nn(a, b):
    return lax.dot_general(a, b, (((1,), (0,)), ((), ())), preferred_element_type=F32)


def dot_nt(a, b):
    return lax.dot_general(a, b, (((1,), (1,)), ((), ())), preferred_element_type=F32)


def kernel(
    n_blk, n_sub, strata,
    users_hbm, items_hbm, counts_hbm, occ_hbm, ratings_ref,
    users_out, items_out,
    users_ref, items_ref, counts_ref, occ_ref,
    low_u, rest_u, low_ut, state_u, part_s, part_r, last_s, last_r,
    own_i, own_rest, slots, rests, hop_s, hop_rest, final_s, final_r, errors, rat, weight,
    in_sem, rat_sem, u_s, u_r, v_s, v_r, i_s, i_r, j_s, j_r, z_s, z_r, y_s, y_r, f_s, f_r, g_s, g_r, p_s, p_r,
):
    n_hi = n_sub // LO
    rows, users = users_ref.shape
    ranks = rows * n_sub
    items = items_ref.shape[1]
    half = items // LO
    width = half // CHUNKS
    pair = LO * rows
    part = users // PARTS
    blk = lax.axis_index("blk")
    me = lax.axis_index("sub")
    hi, lo = me // LO, me % LO

    def at_blk(steps):
        return lax.rem(blk + steps % n_blk, n_blk)

    def at_hi(steps):
        return lax.rem(hi + steps, n_hi)

    def at_lo(steps):
        return lax.rem(lo + steps, LO)

    def sub_of(hi_at, lo_at):
        return hi_at * LO + lo_at

    def rows_of(sub_at):
        return pl.ds(pl.multiple_of(sub_at * rows, rows), rows)

    def pair_of(hi_at):
        return pl.ds(pl.multiple_of(hi_at * pair, pair), pair)

    def send(src, dst, send_sem, recv_sem, blk_at, sub_at):
        copy = pltpu.make_async_remote_copy(
            src_ref=src, dst_ref=dst, send_sem=send_sem, recv_sem=recv_sem,
            device_id={"blk": blk_at, "sub": sub_at}, device_id_type=pl.DeviceIdType.MESH,
        )
        copy.start()
        return copy

    def arrived(dst, recv_sem):
        pltpu.make_async_remote_copy(
            src_ref=dst, dst_ref=dst, send_sem=recv_sem, recv_sem=recv_sem,
            device_id={"blk": blk, "sub": me}, device_id_type=pl.DeviceIdType.MESH,
        ).wait_recv()

    sent = []
    loads = []
    first = []
    for at, (source, target) in enumerate((
        (users_hbm, users_ref), (items_hbm, items_ref), (counts_hbm, counts_ref), (occ_hbm, occ_ref),
    )):
        load = pltpu.make_async_copy(source, target, in_sem.at[at])
        load.start()
        first.append(load)
    for s in range(strata):
        load = pltpu.make_async_copy(
            ratings_ref.at[s, :, pl.ds(pl.multiple_of(lo * half, half), half)],
            rat.at[s], rat_sem.at[s],
        )
        load.start()
        loads.append(load)

    barrier = pltpu.get_barrier_semaphore()
    greeted = [(0, dh, dl) for dh in range(n_hi) for dl in range(LO) if (dh, dl) != (0, 0)]
    for d in sorted({sign * k % n_blk for k in (1,) for sign in (1, -1)} - {0}):
        greeted += [(d, 0, dl) for dl in range(LO)]
    for d, dh, dl in greeted:
        pl.semaphore_signal(
            barrier, inc=1,
            device_id={"blk": at_blk(d), "sub": sub_of(at_hi(dh), at_lo(dl))},
            device_id_type=pl.DeviceIdType.MESH,
        )

    def split(value):
        high = value.astype(BF16)
        return high, (value - high.astype(F32)).astype(BF16)

    for load in first:
        load.wait()
    low_u[rows_of(me), :], rest_u[rows_of(me), :] = split(users_ref[...])
    for h in range(LO):
        for k in range(CHUNKS):
            cols = slice((h * CHUNKS + k) * width, (h * CHUNKS + k + 1) * width)
            own_i[h, k], own_rest[h, k] = split(items_ref[:, cols])
    for k in range(CHUNKS):
        slots[0, k, rows_of(me), :] = own_i[lo, k]
        rests[0, k, rows_of(me), :] = own_rest[lo, k]
    pl.semaphore_wait(barrier, len(greeted))

    mine = low_u.at[rows_of(me), :]
    for dh in range(1, n_hi):
        sent.append(send(mine, mine, u_s.at[dh], u_r.at[me], blk, sub_of(at_hi(dh), lo)))
    sent.append(send(mine, mine, u_s.at[0], u_r.at[me], blk, sub_of(hi, at_lo(1))))
    user_sent = list(sent)
    sent.clear()
    for k in range(CHUNKS):
        at = 0
        for dl in range(LO):
            for dh in range(n_hi):
                if (dh, dl) == (0, 0):
                    continue
                sent.append(send(
                    own_i.at[at_lo(dl), k], slots.at[0, k, rows_of(me), :],
                    i_s.at[k, at], i_r.at[k, me], blk, sub_of(at_hi(dh), at_lo(dl)),
                ))
                at += 1
    mine = rest_u.at[rows_of(me), :]
    for dh in range(1, n_hi):
        sent.append(send(mine, mine, v_s.at[dh], v_r.at[me], blk, sub_of(at_hi(dh), lo)))
    sent.append(send(mine, mine, v_s.at[0], v_r.at[me], blk, sub_of(hi, at_lo(1))))
    for k in range(CHUNKS):
        sent.append(send(
            own_rest.at[at_lo(1), k], rests.at[0, k, rows_of(me), :],
            j_s.at[k], j_r.at[k], blk, sub_of(hi, at_lo(1)),
        ))

    tiles = counts_ref.shape[1]
    group = users // occ_ref.shape[2]
    tile_width = items // tiles
    tile_at = lax.broadcasted_iota(jnp.int32, (tiles, half), 0)
    lane_at = lax.broadcasted_iota(jnp.int32, (tiles, half), 1)
    spread = jnp.where((lane_at + lo * half) // tile_width == tile_at, 1.0, 0.0).astype(BF16)
    position = (lax.broadcasted_iota(jnp.int32, (group, half), 1) % tile_width).astype(F32)

    def make_weight(s):
        for b in range(users // group):
            seen = counts_ref[s, :, b * group:(b + 1) * group].astype(F32).astype(BF16)
            open_tiles = occ_ref[s, :, b:b + 1].astype(F32).astype(BF16)
            seen = lax.dot_general(
                seen, spread * open_tiles, (((0,), (0,)), ((), ())), preferred_element_type=F32
            )
            weight[s, b * group:(b + 1) * group, :] = jnp.where(position < seen, 1.0, 0.0).astype(BF16)

    make_weight(0)
    for dh in range(1, n_hi):
        other = sub_of(at_hi(dh), lo)
        piece = low_u.at[rows_of(other), :]
        arrived(piece, u_r.at[other])
        user_sent.append(send(piece, piece, u_s.at[n_hi - 1 + dh], u_r.at[other], blk, sub_of(hi, at_lo(1))))
    for s in range(1, strata):
        make_weight(s)
    for dh in range(n_hi):
        other = sub_of(at_hi(dh), at_lo(1))
        arrived(low_u.at[rows_of(other), :], u_r.at[other])
    low_ut[...] = low_u[...].T

    def piece_of(hi_at, q):
        piece = pair // PIECES
        return pl.ds(pl.multiple_of(hi_at * pair + q * piece, piece), piece)

    def pass_on(s, k):
        for q in range(PIECES):
            piece = slots.at[s, k, piece_of(hi, q), :]
            arrived(piece, z_r.at[s, k, q])
            for dh in range(1, n_hi):
                sent.append(send(
                    piece, piece, f_s.at[s, k, q, dh], f_r.at[s, k, q, hi], blk, sub_of(at_hi(dh), lo),
                ))

    for s in range(strata):
        last = s == strata - 1
        loads[s].wait()
        for k in range(CHUNKS):
            if s == 0:
                for dh in range(n_hi):
                    for dl in range(LO):
                        if (dh, dl) != (0, 0):
                            other = sub_of(at_hi(dh), at_lo(dl))
                            arrived(slots.at[0, k, rows_of(other), :], i_r.at[k, other])
            else:
                for dh in range(1, n_hi):
                    other = at_hi(dh)
                    for q in range(PIECES):
                        arrived(slots.at[s, k, piece_of(other, q), :], f_r.at[s, k, q, other])
            cols = slice(k * width, (k + 1) * width)
            scores = dot_nn(low_ut[...], slots[s, k])
            error = (scores - rat[s, :, cols].astype(F32)).astype(BF16) * weight[s, :, cols]
            errors[:, cols] = error
            step = step_rate * dot_nn(low_u[pair_of(hi), :], error)
            if s == 0:
                arrived(rests.at[0, k, rows_of(sub_of(hi, at_lo(1))), :], j_r.at[k])
            else:
                arrived(rests.at[s, k, pair_of(hi), :], y_r.at[s, k])
            after = slots[s, k, pair_of(hi), :].astype(F32) + rests[s, k, pair_of(hi), :].astype(F32) - step
            if not last:
                hop_s[s, k], hop_rest[s, k] = split(after)
                for q in range(PIECES):
                    sent.append(send(
                        hop_s.at[s, k, piece_of(0, q), :], slots.at[s + 1, k, piece_of(hi, q), :],
                        z_s.at[s, k, q], z_r.at[s + 1, k, q], at_blk(1), me,
                    ))
            else:
                for h in range(LO):
                    final_s[k, h] = after[h * rows:(h + 1) * rows, :]
                for dl in range(LO):
                    sent.append(send(
                        final_s.at[k, at_lo(dl)], final_r.at[lo, k],
                        g_s.at[k, dl], g_r.at[lo, k], at_blk(1), sub_of(hi, at_lo(dl)),
                    ))
        if not last:
            for k in range(CHUNKS):
                sent.append(send(
                    hop_rest.at[s, k], rests.at[s + 1, k, pair_of(hi), :],
                    y_s.at[s, k], y_r.at[s + 1, k], at_blk(1), me,
                ))
        for p in range(PARTS):
            of_part = slice(p * part, (p + 1) * part)
            total = None
            for k in range(CHUNKS):
                held = slots[s, k] if not last else slots[s, k, pair_of(hi), :]
                grad = dot_nt(held, errors[of_part, k * width:(k + 1) * width])
                total = grad if total is None else total + grad
            if not last:
                part_s[s, p] = total
                sent.append(send(
                    part_s.at[s, p], part_r.at[s, p], p_s.at[s, p], p_r.at[s, p],
                    blk, sub_of(hi, at_lo(1)),
                ))
            else:
                for h in range(LO):
                    last_s[p, h] = total[h * rows:(h + 1) * rows, :]
                sent.append(send(
                    last_s.at[p, at_lo(1)], last_r.at[p], p_s.at[s, p], p_r.at[s, p],
                    blk, sub_of(hi, at_lo(1)),
                ))
        if s == 0:
            for dh in range(1, n_hi):
                other = sub_of(at_hi(dh), lo)
                piece = rest_u.at[rows_of(other), :]
                arrived(piece, v_r.at[other])
                sent.append(send(
                    piece, piece, v_s.at[n_hi - 1 + dh], v_r.at[other], blk, sub_of(hi, at_lo(1)),
                ))
            for dh in range(n_hi):
                other = sub_of(at_hi(dh), at_lo(1))
                arrived(rest_u.at[rows_of(other), :], v_r.at[other])
            for copy in user_sent:
                copy.wait_send()
        if not last:
            pass_on(s + 1, 0)
        for p in range(PARTS):
            of_part = slice(p * part, (p + 1) * part)
            if not last:
                arrived(part_r.at[s, p], p_r.at[s, p])
                before = state_u[:, of_part]
                if s == 0:
                    before = low_u[:, of_part].astype(F32) + rest_u[:, of_part].astype(F32)
                after = before - step_rate * (part_s[s, p] + part_r[s, p])
                state_u[:, of_part] = after
                after = after.astype(BF16)
                low_u[:, of_part] = after
                low_ut[of_part, :] = after.T
                for k in range(1 + p * (CHUNKS - 1) // PARTS, 1 + (p + 1) * (CHUNKS - 1) // PARTS):
                    pass_on(s + 1, k)
            else:
                arrived(last_r.at[p], p_r.at[s, p])
                users_out[:, of_part] = state_u[rows_of(me), of_part] - step_rate * (last_s[p, lo] + last_r[p])

    for dl in range(LO):
        for k in range(CHUNKS):
            arrived(final_r.at[at_lo(dl), k], g_r.at[at_lo(dl), k])
    for h in range(LO):
        for k in range(CHUNKS):
            items_out[:, (h * CHUNKS + k) * width:(h * CHUNKS + k + 1) * width] = final_r[h, k]
    for copy in sent:
        copy.wait_send()


def per_device(n_blk, n_sub, user_factors, item_factors, ratings, counts, occupancy):
    strata, users, items = ratings.shape
    rows = user_factors.shape[0]
    ranks = rows * n_sub
    half = items // LO
    width = half // CHUNKS
    pair = LO * rows
    n_hi = n_sub // LO
    part = users // PARTS
    counts, occupancy = jnp.swapaxes(counts, 1, 2), jnp.swapaxes(occupancy, 1, 2)
    vmem = pl.BlockSpec(memory_space=pltpu.VMEM)
    dma = pltpu.SemaphoreType.DMA
    return pl.pallas_call(
        functools.partial(kernel, n_blk, n_sub, strata),
        out_shape=(
            jax.ShapeDtypeStruct((rows, users), F32),
            jax.ShapeDtypeStruct((rows, items), F32),
        ),
        in_specs=[pl.BlockSpec(memory_space=pltpu.HBM)] * 5,
        out_specs=(vmem, vmem),
        scratch_shapes=[
            pltpu.VMEM(user_factors.shape, F32),
            pltpu.VMEM(item_factors.shape, F32),
            pltpu.VMEM(counts.shape, jnp.int32),
            pltpu.VMEM(occupancy.shape, jnp.int32),
            pltpu.VMEM((ranks, users), BF16),
            pltpu.VMEM((ranks, users), BF16),
            pltpu.VMEM((users, ranks), BF16),
            pltpu.VMEM((ranks, users), F32),
            pltpu.VMEM((strata - 1, PARTS, ranks, part), F32),
            pltpu.VMEM((strata - 1, PARTS, ranks, part), F32),
            pltpu.VMEM((PARTS, LO, rows, part), F32),
            pltpu.VMEM((PARTS, rows, part), F32),
            pltpu.VMEM((LO, CHUNKS, rows, width), BF16),
            pltpu.VMEM((LO, CHUNKS, rows, width), BF16),
            pltpu.VMEM((strata, CHUNKS, ranks, width), BF16),
            pltpu.VMEM((strata, CHUNKS, ranks, width), BF16),
            pltpu.VMEM((strata - 1, CHUNKS, pair, width), BF16),
            pltpu.VMEM((strata - 1, CHUNKS, pair, width), BF16),
            pltpu.VMEM((CHUNKS, LO, rows, width), F32),
            pltpu.VMEM((LO, CHUNKS, rows, width), F32),
            pltpu.VMEM((users, half), BF16),
            pltpu.VMEM((strata, users, half), BF16),
            pltpu.VMEM((strata, users, half), BF16),
            dma((4,)),
            dma((strata,)),
            dma((2 * n_hi,)),
            dma((n_sub,)),
            dma((2 * n_hi,)),
            dma((n_sub,)),
            dma((CHUNKS, n_sub)),
            dma((CHUNKS, n_sub)),
            dma((CHUNKS,)),
            dma((CHUNKS,)),
            dma((strata, CHUNKS, PIECES)),
            dma((strata, CHUNKS, PIECES)),
            dma((strata, CHUNKS)),
            dma((strata, CHUNKS)),
            dma((strata, CHUNKS, PIECES, n_hi)),
            dma((strata, CHUNKS, PIECES, n_hi)),
            dma((CHUNKS, LO)),
            dma((LO, CHUNKS)),
            dma((strata, PARTS)),
            dma((strata, PARTS)),
        ],
        compiler_params=pltpu.CompilerParams(
            collective_id=0, has_side_effects=True, vmem_limit_bytes=52 * 2**20
        ),
        cost_estimate=pl.CostEstimate(
            flops=6 * strata * ranks * users * half, transcendentals=0,
            bytes_accessed=strata * users * items * 2,
        ),
    )(user_factors, item_factors, counts, occupancy, ratings)


def solution(mesh):
    return jax.shard_map(
        functools.partial(per_device, mesh.shape["blk"], mesh.shape["sub"]),
        mesh=mesh,
        in_specs=(
            P("sub", ("groups", "blk")),
            P("sub", ("groups", "blk")),
            P(None, ("groups", "blk"), None),
            P(None, ("groups", "blk"), None),
            P(None, ("groups", "blk"), None),
        ),
        out_specs=(P("sub", ("groups", "blk")), P("sub", ("groups", "blk"))),
        check_vma=False,
    )
```
